32 devices in a mesh: groups: 2 (over x), expert: 16 (over z, y, core).
Axes of the slice: x: 2, y: 2, z: 4, core: 2. Of those that a mesh axis runs over, the one named last changes fastest.
Arguments:
- tokens: bfloat16 [1024, 7168], P(('groups', 'expert')), parts along dimension 0, may hold values from -6 to 6
- expert_ids: int32 [1024, 8], P(('groups', 'expert')), parts along dimension 0, may hold values from 0 to 255, as said below
- replica: int32 [1024, 8], P(('groups', 'expert')), parts along dimension 0, may hold values from 0 to 1
- gate_weights: float32 [1024, 8], P(('groups', 'expert')), parts along dimension 0, may hold values from 0.1 to 0.6
- slot_table: int32 [512, 2], P('groups'), parts along dimension 0, may hold values from 0 to 2, as said below
- gate_pieces: bfloat16 [32, 7168, 256], P(('groups', 'expert')), parts along dimension 0, as said below
- up_pieces: bfloat16 [32, 7168, 256], P(('groups', 'expert')), parts along dimension 0, as said below
- down_pieces: bfloat16 [32, 256, 7168], P(('groups', 'expert')), parts along dimension 0, as said below
Outputs:
- routed_output: bfloat16 [1024, 7168], P(('groups', 'expert')), parts along dimension 0
The draws below stay inside these ranges and needn't reach their ends.
There are 2 independent parts, one for each index of `groups`. The reference program is written for one: setup_inputs(seed, part) draws one part's arguments, and reference() takes and returns one part's arrays. A program takes and returns all parts, laid end to end along the dimension named above; each array names one. Nothing has to cross between parts.
Inputs may be any that keep to these rules, and one draw needn't show every extreme that they name: `expert_ids`: each row names 8 different experts. `slot_table`: row e holds the copies hosting expert e for replicas 0 and 1, two different copies, or 2 twice where e is not hosted; every copy hosts exactly one expert, and 1 experts are hosted. `gate_pieces`: slots of copies that host the same expert hold equal weights. `up_pieces`: slots of copies that host the same expert hold equal weights. `down_pieces`: slots of copies that host the same expert hold equal weights.
All inputs are finite; a program needn't handle non-finite values.
Results may differ from the reference program's by a relative error of at most 0.0057.
Values may be sent and summed in bfloat16 or wider, within the bound.
No kernel may reach another device: no remote copies, remote signals or barrier semaphores. Data moves between devices by JAX's collectives and lax.ppermute only.
A program may use at most 128 MiB of HBM per device.

```python
import jax
import jax.numpy as jnp
from jax import lax

D = 7168
FF = 2048
SPECIALIST_COUNT = 256
TOPK = 8
PIECES = 8
TOK_DEV = 32
CAP = 12
COPIES = 2
RESIDENT = 1
ROWS = 512
N_EXPERT = 16


def hosting(key):
    order = jax.random.permutation(jax.random.fold_in(key, 101), SPECIALIST_COUNT)
    hot_experts = order[:RESIDENT].astype(jnp.int32)
    copy_order = jax.random.permutation(jax.random.fold_in(key, 102), COPIES).astype(jnp.int32)
    host_of_copy = jnp.zeros((COPIES,), jnp.int32).at[copy_order].set(jnp.arange(COPIES, dtype=jnp.int32) // 2)
    return (hot_experts, copy_order, host_of_copy)


def draw_slot_table(key, part):
    hot_experts, copy_order, host_of_copy = hosting(key)
    table = jnp.full((SPECIALIST_COUNT, 2), COPIES, jnp.int32)
    table = table.at[hot_experts, 0].set(copy_order[0::2])
    table = table.at[hot_experts, 1].set(copy_order[1::2])
    return table


def draw_expert_ids(key, part):
    hot_experts, copy_order, host_of_copy = hosting(key)
    key = jax.random.fold_in(key, 2)
    resident_range = jnp.arange(RESIDENT, dtype=jnp.int32)
    thresholds = 900 - 550 * resident_range // max(RESIDENT - 1, 1)
    draws = jax.random.randint(jax.random.fold_in(key, 3), (ROWS, RESIDENT), 0, 1000)
    admission_filter = (draws < thresholds[None, :]).astype(jnp.int32)
    specialist_extent = jnp.arange(SPECIALIST_COUNT, dtype=jnp.int32)
    specialist_flags = (hot_experts[:, None] == specialist_extent[None, :]).astype(jnp.int32)
    additive_preference = jnp.sum(admission_filter[:, :, None] * specialist_flags[None, :, :], axis=1) * 8192
    starting_shift = jax.random.randint(jax.random.fold_in(key, 4), (ROWS, SPECIALIST_COUNT), 0, 4096)
    gating_logits = (starting_shift + additive_preference) * SPECIALIST_COUNT + specialist_extent[None, :]
    return lax.top_k(gating_logits, TOPK)[1].astype(jnp.int32)


def spread_weights(key, rows_in, rows_out, split_last):
    hot_experts, copy_order, host_of_copy = hosting(key)
    starting_shift = jax.random.truncated_normal(key, -4.0, 4.0, (RESIDENT, rows_in, rows_out), jnp.float32) * rows_in ** (-0.5)
    if split_last:
        pieces = starting_shift.reshape(RESIDENT, rows_in, PIECES, rows_out // PIECES).transpose(0, 2, 1, 3)
    else:
        pieces = starting_shift.reshape(RESIDENT, PIECES, rows_in // PIECES, rows_out)
    placed = pieces[host_of_copy]
    return placed.reshape((N_EXPERT,) + placed.shape[2:]).astype(jnp.bfloat16)


def draw_gate_pieces(key, part):
    return spread_weights(jax.random.fold_in(key, 11), D, FF, True)


def draw_up_pieces(key, part):
    return spread_weights(jax.random.fold_in(key, 12), D, FF, True)


def draw_down_pieces(key, part):
    return spread_weights(jax.random.fold_in(key, 13), FF, D, False)


def set_ends(array, own_key, smallest, high):
    spot = [jax.random.randint(jax.random.fold_in(own_key, axis), (), 0, length) for axis, length in enumerate(array.shape)]
    widest = array.shape.index(max(array.shape))
    next_to = spot[:widest] + [(spot[widest] + 1) % array.shape[widest]] + spot[widest + 1:]
    return array.at[tuple(spot)].set(smallest).at[tuple(next_to)].set(high)


def levels(key, dims, cuts, smallest, top_value):
    def one(dim, shards_of):
        steps = jax.random.uniform(jax.random.fold_in(jax.random.fold_in(key, 6), dim), (shards_of,), jnp.float32, smallest / len(cuts), top_value / len(cuts))
        return jnp.repeat(jnp.exp(steps), dims[dim] // shards_of).reshape((-1,) + (1,) * (len(dims) - dim - 1))

    factor_of = one(*cuts[0])
    for cut in cuts[1:]:
        factor_of = factor_of * one(*cut)
    return factor_of


def bell_draw(rng, shape, spread, reach, split=(), kind=jnp.bfloat16):
    entries = jax.random.normal(rng, shape, jnp.float32) * spread
    if len(split) > 0:
        entries = levels(rng, shape, split, -0.22, 0.18) * entries
    return jnp.clip(entries, min=-reach, max=reach).astype(kind)


def setup_inputs(seed: int = 0, part: int = 0) -> dict:
    splits = jax.random.split(jax.random.key(seed), 9)
    part_splits = jax.random.split(jax.random.fold_in(splits[8], part), 9)
    tokens = bell_draw(part_splits[0], (ROWS, D), 1.0, 6.0, ((0, 16),))
    expert_ids = draw_expert_ids(jax.random.fold_in(jax.random.fold_in(splits[8], part), 71), part)
    replica = set_ends(jax.random.randint(part_splits[2], (ROWS, TOPK), 0, 2), jax.random.fold_in(part_splits[2], 1), 0, 1).astype(jnp.int32)
    gate_weights = jnp.clip(0.1 + 0.5 * jax.random.uniform(part_splits[3], (ROWS, TOPK), jnp.float32) ** levels(part_splits[3], (ROWS, TOPK), ((0, 16),), -0.2, 0.2), 0.1, 0.6)
    slot_table = draw_slot_table(jax.random.fold_in(jax.random.fold_in(splits[8], part), 71), part)
    gate_pieces = draw_gate_pieces(jax.random.fold_in(jax.random.fold_in(splits[8], part), 71), part)
    up_pieces = draw_up_pieces(jax.random.fold_in(jax.random.fold_in(splits[8], part), 71), part)
    down_pieces = draw_down_pieces(jax.random.fold_in(jax.random.fold_in(splits[8], part), 71), part)
    return dict(tokens=tokens, expert_ids=expert_ids, replica=replica, gate_weights=gate_weights, slot_table=slot_table, gate_pieces=gate_pieces, up_pieces=up_pieces, down_pieces=down_pieces)


def reference(tokens, expert_ids, replica, gate_weights, slot_table, gate_pieces, up_pieces, down_pieces):
    copy_range = jnp.arange(COPIES, dtype=jnp.int32)
    targets = slot_table[expert_ids, replica]
    members = (targets[:, :, None] == copy_range[None, None, :]).astype(jnp.int32)
    routed = jnp.sum(members, axis=1).reshape(N_EXPERT, TOK_DEV, COPIES)
    position = jnp.cumsum(routed, axis=1) - routed
    retained = routed * (position < CAP).astype(jnp.int32)
    slot_range = jnp.arange(CAP, dtype=jnp.int32)
    chosen = retained[:, :, :, None] * (position[:, :, :, None] == slot_range[None, None, None, :]).astype(jnp.int32)
    row_range = jnp.arange(TOK_DEV, dtype=jnp.int32)
    block_start = jnp.arange(N_EXPERT, dtype=jnp.int32) * TOK_DEV
    sources = jnp.sum(chosen * row_range[None, :, None, None], axis=1) + block_start[:, None, None]
    filled = jnp.sum(chosen, axis=1)
    slot_copy = jnp.arange(N_EXPERT, dtype=jnp.int32) // PIECES

    def one_slot(items):
        gate_part, up_part, down_part, copy_index = items
        row_index = jnp.take(sources, copy_index, axis=1).reshape(-1)
        live_rows = jnp.take(filled, copy_index, axis=1).reshape(-1)
        inputs = tokens[row_index] * live_rows[:, None].astype(tokens.dtype)
        gate_act = jnp.dot(inputs, gate_part, preferred_element_type=jnp.float32)
        up_act = jnp.dot(inputs, up_part, preferred_element_type=jnp.float32)
        hidden = (jax.nn.silu(gate_act) * up_act).astype(jnp.bfloat16)
        return jnp.dot(hidden, down_part, preferred_element_type=jnp.float32).astype(jnp.bfloat16)

    partial_rows = lax.map(one_slot, (gate_pieces, up_pieces, down_pieces, slot_copy))
    combined = jnp.sum(partial_rows.reshape(COPIES, PIECES, N_EXPERT * CAP, D).astype(jnp.float32), axis=1)

    position_rows = position.reshape(ROWS, COPIES)
    retained_rows = retained.reshape(ROWS, COPIES)
    hosted = (targets < COPIES).astype(jnp.int32)
    safe_copy = jnp.minimum(targets, COPIES - 1)
    slot_place = jnp.minimum(jnp.take_along_axis(position_rows, safe_copy, axis=1), CAP - 1)
    live_choice = jnp.take_along_axis(retained_rows, safe_copy, axis=1) * hosted
    row_block = (jnp.arange(ROWS, dtype=jnp.int32) // TOK_DEV)[:, None]
    flat_index = row_block * CAP + slot_place
    total = jnp.zeros((ROWS, D), jnp.float32)
    for column in range(TOPK):
        values = combined[safe_copy[:, column], flat_index[:, column]]
        weight = gate_weights[:, column] * live_choice[:, column].astype(jnp.float32)
        total = total + weight[:, None] * values
    return total.astype(jnp.bfloat16)
```

```python
import functools

import jax
import jax.numpy as jnp
from jax import lax
from jax.experimental import pallas as pl
from jax.experimental.pallas import tpu as pltpu
from jax.sharding import PartitionSpec as P

PIECES = 8
CAP = 12
VMEM_LIMIT = 56 * 1024 * 1024


def expert_rows(arrived, gate_part, up_part, down_part):
    flattened = arrived.reshape(-1, arrived.shape[-1])
    gate_act = jnp.dot(flattened, gate_part, preferred_element_type=jnp.float32)
    up_act = jnp.dot(flattened, up_part, preferred_element_type=jnp.float32)
    hidden = (jax.nn.silu(gate_act) * up_act).astype(jnp.bfloat16)
    result = jnp.dot(hidden, down_part, preferred_element_type=jnp.float32).astype(jnp.bfloat16)
    return result.reshape(arrived.shape[:-1] + (down_part.shape[1],))


def any_copies(
    tokens, expert_ids, replica, gate_weights, slot_table, gate_pieces, up_pieces, down_pieces
):
    devices = lax.axis_size("expert")
    copies = devices // PIECES
    width = tokens.shape[1]
    specialist_extent = jnp.arange(slot_table.shape[0], dtype=jnp.int32)
    matches = (expert_ids[:, :, None] == specialist_extent[None, None, :]).astype(jnp.int32)
    per_replica = jnp.where(
        replica[:, :, None] == 0, slot_table[:, 0][None, None, :], slot_table[:, 1][None, None, :]
    )
    targets = jnp.sum(matches * per_replica, axis=2)
    copy_range = jnp.arange(copies, dtype=jnp.int32)
    members = (targets[:, :, None] == copy_range[None, None, :]).astype(jnp.int32)
    routed = jnp.sum(members, axis=1)
    position = jnp.cumsum(routed, axis=0) - routed
    retained = routed * (position < CAP).astype(jnp.int32)
    gate_copy = jnp.sum(gate_weights[:, :, None] * members.astype(jnp.float32), axis=1)
    slot_range = jnp.arange(CAP, dtype=jnp.int32)
    chosen_rows = retained.T[:, None, :] * (
        position.T[:, None, :] == slot_range[None, :, None]
    ).astype(jnp.int32)
    send_rows = jnp.einsum(
        "cjt,td->cjd", chosen_rows.astype(jnp.bfloat16), tokens, preferred_element_type=jnp.float32
    ).astype(jnp.bfloat16)
    gate_part = gate_pieces[0]
    up_part = up_pieces[0]
    down_part = down_pieces[0]
    outgoing = jnp.broadcast_to(send_rows[:, None], (copies, PIECES, CAP, width)).reshape(
        devices, CAP, width
    )
    arrived = lax.all_to_all(outgoing, "expert", split_axis=0, concat_axis=0, tiled=True)
    produced = expert_rows(arrived, gate_part, up_part, down_part)
    returned = lax.all_to_all(produced, "expert", split_axis=0, concat_axis=0, tiled=True)
    combined = jnp.sum(returned.reshape(copies, PIECES, CAP, width).astype(jnp.float32), axis=1)
    weighting = chosen_rows.astype(jnp.float32) * gate_copy.T[:, None, :]
    total = jnp.einsum("cjt,cjd->td", weighting, combined, precision=lax.Precision.HIGHEST)
    return total.astype(jnp.bfloat16)


def slots_of(ids, rep, table):
    experts = lax.broadcasted_iota(jnp.int32, table.shape, 1)
    here = table < 2
    first = jnp.sum(jnp.where(here, table, 0)[0:1], axis=1, keepdims=True)
    hosted = jnp.sum(jnp.where(here, experts, 0)[0:1], axis=1, keepdims=True)
    hit = ids == hosted
    copy = jnp.where(rep == 0, first, 1 - first)
    count = ids.shape[1]
    to = [jnp.sum(jnp.where(hit & (copy == c), 1.0, 0.0), axis=0, keepdims=True) for c in range(2)]
    earlier = (
        lax.broadcasted_iota(jnp.int32, (count, count), 0)
        < lax.broadcasted_iota(jnp.int32, (count, count), 1)
    ).astype(jnp.float32)
    slot = jnp.full((1, count), -1, jnp.int32)
    for c in range(2):
        routed = jnp.broadcast_to(to[c], (8, count))
        position = jnp.dot(routed, earlier, preferred_element_type=jnp.float32)[0:1]
        position = position.astype(jnp.int32)
        keep = (to[c] > 0.5) & (position < CAP)
        slot = jnp.where(keep, position + c * CAP, slot)
    return slot, hit


def pick_kernel(tok_ref, ids_ref, rep_ref, table_ref, low_ref, high_ref):
    slot, _ = slots_of(ids_ref[...], rep_ref[...], table_ref[...])
    count = slot.shape[1]
    chosen = lax.broadcasted_iota(jnp.int32, (2 * CAP, count), 0) == slot
    chosen = chosen.astype(jnp.bfloat16)
    half = low_ref.shape[1]
    low_ref[...] = jnp.dot(
        chosen, tok_ref[:, :half], preferred_element_type=jnp.float32
    ).astype(jnp.bfloat16)
    high_ref[...] = jnp.dot(
        chosen, tok_ref[:, half:], preferred_element_type=jnp.float32
    ).astype(jnp.bfloat16)


def expert_kernel(*refs):
    x_refs = refs[:16]
    gate_ref, up_ref, down_ref, mine_ref, other_ref, x_all = refs[16:]
    rows = x_refs[0].shape[0]
    half = x_refs[0].shape[1]
    for i in range(8):
        x_all[i * rows : (i + 1) * rows, :half] = x_refs[2 * i][...]
        x_all[i * rows : (i + 1) * rows, half:] = x_refs[2 * i + 1][...]
    x = x_all[...]
    gate = jnp.dot(x, gate_ref[...], preferred_element_type=jnp.float32)
    up = jnp.dot(x, up_ref[...], preferred_element_type=jnp.float32)
    hidden = (gate / (1.0 + jnp.exp(-gate)) * up).astype(jnp.bfloat16)
    out = jnp.dot(hidden, down_ref[...], preferred_element_type=jnp.float32).astype(jnp.bfloat16)
    mine_ref[...] = out[: 4 * rows]
    other_ref[...] = out[4 * rows :]


def combine_kernel(own_ref, y_ref, z_ref, ids_ref, rep_ref, table_ref, w_ref, out_ref):
    slot, hit = slots_of(ids_ref[...], rep_ref[...], table_ref[...])
    weight = jnp.sum(jnp.where(hit, w_ref[...], 0.0), axis=0, keepdims=True)
    count = slot.shape[1]
    chosen = lax.broadcasted_iota(jnp.int32, (2 * CAP, count), 0) == slot
    spread = jnp.where(chosen, weight, 0.0)
    spread_hi = spread.astype(jnp.bfloat16)
    spread_lo = (spread - spread_hi.astype(jnp.float32)).astype(jnp.bfloat16)
    total = own_ref[...].astype(jnp.float32) + y_ref[...].astype(jnp.float32)
    total = total + z_ref[...].astype(jnp.float32)
    total_hi = total.astype(jnp.bfloat16)
    total_lo = (total - total_hi.astype(jnp.float32)).astype(jnp.bfloat16)
    dims = (((0,), (0,)), ((), ()))
    dot = functools.partial(
        lax.dot_general, dimension_numbers=dims, preferred_element_type=jnp.float32
    )
    out = dot(spread_hi, total_hi) + (dot(spread_hi, total_lo) + dot(spread_lo, total_hi))
    out_ref[...] = out.astype(jnp.bfloat16)


def two_copies(
    tokens, expert_ids, replica, gate_weights, slot_table, gate_pieces, up_pieces, down_pieces
):
    devices = lax.axis_size("expert")
    count, width = tokens.shape
    half = width // 2
    rows = 2 * CAP
    bf16 = jnp.bfloat16

    def swap(a, bit):
        return lax.ppermute(a, "expert", [(i, i ^ bit) for i in range(devices)])

    params = pltpu.CompilerParams(vmem_limit_bytes=VMEM_LIMIT)
    ids, rep, table, weights = expert_ids.T, replica.T, slot_table.T, gate_weights.T
    low, high = pl.pallas_call(
        pick_kernel,
        out_shape=[jax.ShapeDtypeStruct((rows, half), bf16)] * 2,
        compiler_params=params,
    )(tokens, ids, rep, table)
    y_low, z_high = swap(low, 2), swap(high, 4)
    y_high, z_low = swap(high, 2), swap(low, 4)
    d_low, d_high = swap(y_low, 4), swap(z_high, 2)
    held = [low, high, y_low, y_high, z_low, z_high, d_low, d_high]
    partner = [swap(a, 1) for a in held]
    mine, other = pl.pallas_call(
        expert_kernel,
        out_shape=[jax.ShapeDtypeStruct((4 * rows, width), bf16)] * 2,
        scratch_shapes=[pltpu.VMEM((8 * rows, width), bf16)],
        compiler_params=params,
    )(*held, *partner, gate_pieces[0], up_pieces[0], down_pieces[0])
    met = swap(other, 1)
    total = (mine.astype(jnp.float32) + met.astype(jnp.float32)).astype(bf16)
    own, to_y, to_z, to_d = (total[i * rows : (i + 1) * rows] for i in range(4))
    from_y, from_z = swap(to_d[:, :half], 2), swap(to_d[:, half:], 4)
    f32 = jnp.float32
    to_z = jnp.concatenate(
        [(to_z[:, :half].astype(f32) + from_y.astype(f32)).astype(bf16), to_z[:, half:]], axis=1
    )
    to_y = jnp.concatenate(
        [to_y[:, :half], (to_y[:, half:].astype(f32) + from_z.astype(f32)).astype(bf16)], axis=1
    )
    got_y, got_z = swap(to_y, 2), swap(to_z, 4)
    return pl.pallas_call(
        combine_kernel,
        out_shape=jax.ShapeDtypeStruct((count, width), bf16),
        compiler_params=params,
    )(own, got_y, got_z, ids, rep, table, weights)


def solution(mesh):
    placed = (
        P(("groups", "expert"), None),
        P(("groups", "expert"), None),
        P(("groups", "expert"), None),
        P(("groups", "expert"), None),
        P("groups", None),
        P(("groups", "expert"), None, None),
        P(("groups", "expert"), None, None),
        P(("groups", "expert"), None, None),
    )
    return jax.shard_map(
        two_copies if mesh.shape["expert"] == 2 * PIECES else any_copies,
        mesh=mesh,
        in_specs=placed,
        out_specs=P(("groups", "expert"), None),
        check_vma=False,
    )
```

```python
import functools

import jax
import jax.numpy as jnp
from jax import lax
from jax.experimental import pallas as pl
from jax.experimental.pallas import tpu as pltpu
from jax.sharding import PartitionSpec as P

PIECES = 8
CAP = 12


def within(mib):
    return pltpu.CompilerParams(vmem_limit_bytes=mib * 2**20)


def expert_rows(arrived, gate_part, up_part, down_part):
    flattened = arrived.reshape(-1, arrived.shape[-1])
    gate_act = jnp.dot(flattened, gate_part, preferred_element_type=jnp.float32)
    up_act = jnp.dot(flattened, up_part, preferred_element_type=jnp.float32)
    hidden = (jax.nn.silu(gate_act) * up_act).astype(jnp.bfloat16)
    result = jnp.dot(hidden, down_part, preferred_element_type=jnp.float32).astype(jnp.bfloat16)
    return result.reshape(arrived.shape[:-1] + (down_part.shape[1],))


def any_copies(
    tokens, expert_ids, replica, gate_weights, slot_table, gate_pieces, up_pieces, down_pieces
):
    devices = lax.axis_size("expert")
    copies = devices // PIECES
    width = tokens.shape[1]
    specialist_extent = jnp.arange(slot_table.shape[0], dtype=jnp.int32)
    matches = (expert_ids[:, :, None] == specialist_extent[None, None, :]).astype(jnp.int32)
    per_replica = jnp.where(
        replica[:, :, None] == 0, slot_table[:, 0][None, None, :], slot_table[:, 1][None, None, :]
    )
    targets = jnp.sum(matches * per_replica, axis=2)
    copy_range = jnp.arange(copies, dtype=jnp.int32)
    members = (targets[:, :, None] == copy_range[None, None, :]).astype(jnp.int32)
    routed = jnp.sum(members, axis=1)
    position = jnp.cumsum(routed, axis=0) - routed
    retained = routed * (position < CAP).astype(jnp.int32)
    gate_copy = jnp.sum(gate_weights[:, :, None] * members.astype(jnp.float32), axis=1)
    slot_range = jnp.arange(CAP, dtype=jnp.int32)
    chosen_rows = retained.T[:, None, :] * (
        position.T[:, None, :] == slot_range[None, :, None]
    ).astype(jnp.int32)
    send_rows = jnp.einsum(
        "cjt,td->cjd", chosen_rows.astype(jnp.bfloat16), tokens, preferred_element_type=jnp.float32
    ).astype(jnp.bfloat16)
    gate_part = gate_pieces[0]
    up_part = up_pieces[0]
    down_part = down_pieces[0]
    outgoing = jnp.broadcast_to(send_rows[:, None], (copies, PIECES, CAP, width)).reshape(
        devices, CAP, width
    )
    arrived = lax.all_to_all(outgoing, "expert", split_axis=0, concat_axis=0, tiled=True)
    produced = expert_rows(arrived, gate_part, up_part, down_part)
    returned = lax.all_to_all(produced, "expert", split_axis=0, concat_axis=0, tiled=True)
    combined = jnp.sum(returned.reshape(copies, PIECES, CAP, width).astype(jnp.float32), axis=1)
    weighting = chosen_rows.astype(jnp.float32) * gate_copy.T[:, None, :]
    total = jnp.einsum("cjt,cjd->td", weighting, combined, precision=lax.Precision.HIGHEST)
    return total.astype(jnp.bfloat16)


def slots_of(ids, rep, table):
    experts = lax.broadcasted_iota(jnp.int32, table.shape, 1)
    here = table < 2
    first = jnp.sum(jnp.where(here, table, 0)[0:1], axis=1, keepdims=True)
    hosted = jnp.sum(jnp.where(here, experts, 0)[0:1], axis=1, keepdims=True)
    hit = ids == hosted
    copy = jnp.where(rep == 0, first, 1 - first)
    count = ids.shape[1]
    to = [jnp.sum(jnp.where(hit & (copy == c), 1.0, 0.0), axis=0, keepdims=True) for c in range(2)]
    earlier = (
        lax.broadcasted_iota(jnp.int32, (count, count), 0)
        < lax.broadcasted_iota(jnp.int32, (count, count), 1)
    ).astype(jnp.float32)
    slot = jnp.full((1, count), -1, jnp.int32)
    for c in range(2):
        routed = jnp.broadcast_to(to[c], (8, count))
        position = jnp.dot(routed, earlier, preferred_element_type=jnp.float32)[0:1]
        position = position.astype(jnp.int32)
        keep = (to[c] > 0.5) & (position < CAP)
        slot = jnp.where(keep, position + c * CAP, slot)
    return slot, hit


def copies_of(refs, sems):
    copies = [pltpu.make_async_copy(s, t, sems.at[i]) for i, (s, t) in enumerate(refs)]
    for copy in copies:
        copy.start()
    return copies


def pick_kernel(
    tok_hbm, ids_hbm, rep_hbm, table_hbm, w_hbm, out_ref, spread_ref,
    tok_ref, ids_ref, rep_ref, table_ref, w_ref, sems,
):
    copies = copies_of(
        [
            (ids_hbm, ids_ref),
            (rep_hbm, rep_ref),
            (table_hbm, table_ref),
            (w_hbm, w_ref),
            (tok_hbm, tok_ref),
        ],
        sems,
    )
    for copy in copies[:4]:
        copy.wait()
    slot, hit = slots_of(ids_ref[...], rep_ref[...], table_ref[...])
    weight = jnp.sum(jnp.where(hit, w_ref[...], 0.0), axis=0, keepdims=True)
    count = slot.shape[1]
    chosen = lax.broadcasted_iota(jnp.int32, (2 * CAP, count), 0) == slot
    spread_ref[...] = jnp.where(chosen, weight, 0.0)
    copies[4].wait()
    out_ref[...] = jnp.dot(
        chosen.astype(jnp.bfloat16), tok_ref[...], preferred_element_type=jnp.float32
    ).astype(jnp.bfloat16)


def activation(gate, up):
    return (gate / (1.0 + jnp.exp(-gate)) * up).astype(jnp.bfloat16)


def load_kernel(gate_hbm, up_hbm, down_hbm, gate_ref, up_ref, down_ref, sems):
    steps = sems.shape[1]
    pairs = []
    for source, target in ((gate_hbm, gate_ref), (up_hbm, up_ref), (down_hbm, down_ref)):
        step = source.shape[0] // steps
        for i in range(steps):
            part = pl.ds(i * step, step)
            pairs.append((source.at[part], target.at[part]))
    copies = [
        pltpu.make_async_copy(s, t, sems.at[i // steps, i % steps])
        for i, (s, t) in enumerate(pairs)
    ]
    for copy in copies:
        copy.start()
    for copy in copies:
        copy.wait()


def hold_kernel(*refs):
    pass


def expert_kernel(*refs):
    gate_ref, up_ref, down_ref, mine_ref, other_ref, x_all = refs[-6:]
    rows = refs[0].shape[0]
    for i, ref in enumerate(refs[:-6]):
        x_all[i * rows : (i + 1) * rows] = ref[...]
    x = x_all[...]
    gate = jnp.dot(x, gate_ref[...], preferred_element_type=jnp.float32)
    up = jnp.dot(x, up_ref[...], preferred_element_type=jnp.float32)
    hidden = activation(gate, up)
    out = jnp.dot(hidden, down_ref[...], preferred_element_type=jnp.float32).astype(jnp.bfloat16)
    mine_ref[...] = out[: mine_ref.shape[0]]
    other_ref[...] = out[mine_ref.shape[0] :]


def combine_kernel(mine_ref, met_ref, first_ref, second_ref, spread_ref, out_ref):
    spread = spread_ref[...]
    spread_hi = spread.astype(jnp.bfloat16)
    spread_lo = (spread - spread_hi.astype(jnp.float32)).astype(jnp.bfloat16)
    dims = (((0,), (0,)), ((), ()))
    dot = functools.partial(
        lax.dot_general, dimension_numbers=dims, preferred_element_type=jnp.float32
    )
    rows = first_ref.shape[0]
    total = mine_ref[:rows].astype(jnp.float32) + met_ref[:rows].astype(jnp.float32)
    for ref in (first_ref, second_ref):
        total = total + ref[...].astype(jnp.float32)
    total_hi = total.astype(jnp.bfloat16)
    total_lo = (total - total_hi.astype(jnp.float32)).astype(jnp.bfloat16)
    out = dot(spread_hi, total_hi) + (dot(spread_hi, total_lo) + dot(spread_lo, total_hi))
    out_ref[...] = out.astype(jnp.bfloat16)


def two_copies(
    tokens, expert_ids, replica, gate_weights, slot_table, gate_pieces, up_pieces, down_pieces
):
    devices = lax.axis_size("expert")
    count, width = tokens.shape
    rows = 2 * CAP
    hidden = gate_pieces.shape[2]
    bf16, f32 = jnp.bfloat16, jnp.float32
    in_hbm = pl.BlockSpec(memory_space=pltpu.HBM)
    in_vmem = pl.BlockSpec(memory_space=pltpu.VMEM)

    def partner(a):
        return lax.ppermute(a, "expert", [(i, i ^ 1) for i in range(devices)])

    def cross(a):
        return lax.ppermute(a, "expert", [(i, i ^ (4 if i % 2 else 2)) for i in range(devices)])

    def cross_back(a):
        return lax.ppermute(a, "expert", [(i, i ^ (2 if i % 2 else 4)) for i in range(devices)])

    def add(a, b):
        return (a.astype(f32) + b.astype(f32)).astype(bf16)

    def cost(total):
        return pl.CostEstimate(
            flops=6 * total * width * hidden, bytes_accessed=6 * width * hidden, transcendentals=0
        )

    small = [expert_ids.T, replica.T, slot_table.T, gate_weights.T]
    own, spread = pl.pallas_call(
        pick_kernel,
        out_shape=[
            jax.ShapeDtypeStruct((rows, width), bf16),
            jax.ShapeDtypeStruct((rows, count), f32),
        ],
        in_specs=[in_hbm] * 5,
        scratch_shapes=[pltpu.VMEM(a.shape, a.dtype) for a in [tokens] + small]
        + [pltpu.SemaphoreType.DMA((5,))],
        compiler_params=within(56),
    )(tokens, *small)
    gate, up, down = pl.pallas_call(
        load_kernel,
        out_shape=[
            jax.ShapeDtypeStruct(a.shape[1:], bf16) for a in (gate_pieces, up_pieces, down_pieces)
        ],
        in_specs=[in_hbm] * 3,
        out_specs=[in_vmem] * 3,
        scratch_shapes=[pltpu.SemaphoreType.DMA((3, 8))],
        compiler_params=within(40),
        cost_estimate=cost(2 * rows),
    )(gate_pieces[0], up_pieces[0], down_pieces[0])

    def after(done, *arrays):
        anywhere = pl.BlockSpec(memory_space=pl.ANY)
        return pl.pallas_call(
            hold_kernel,
            out_shape=[jax.ShapeDtypeStruct(a.shape, a.dtype) for a in arrays],
            in_specs=[anywhere] * (1 + len(arrays)),
            out_specs=[anywhere] * len(arrays),
            input_output_aliases={1 + i: i for i in range(len(arrays))},
            compiler_params=within(1),
        )(done, *arrays)

    def experts(blocks):
        total = 2 * rows * len(blocks)
        return pl.pallas_call(
            expert_kernel,
            out_shape=[jax.ShapeDtypeStruct((total // 2, width), bf16)] * 2,
            scratch_shapes=[pltpu.VMEM((total, width), bf16)],
            compiler_params=within(24),
            cost_estimate=cost(total),
        )(*blocks, *[partner(a) for a in blocks], gate, up, down)

    (near,) = after(gate, cross(own))
    far = cross_back(near)
    side = cross_back(own)
    far_mine, far_other = experts([far])
    far_met = partner(far_other)
    (side,) = after(far_mine, side)
    mine, other = experts([own, near, side])
    met = partner(other)
    block = [slice(i * rows, (i + 1) * rows) for i in range(3)]
    passing = cross_back(add(far_mine, far_met))
    got_side = cross_back(add(mine[block[2]], met[block[2]]))
    to_near = mine[block[1]].astype(f32) + met[block[1]].astype(f32) + passing.astype(f32)
    got_near = cross(to_near.astype(bf16))
    return pl.pallas_call(
        combine_kernel,
        out_shape=jax.ShapeDtypeStruct((count, width), bf16),
        compiler_params=within(24),
    )(mine, met, got_side, got_near, spread)


def solution(mesh):
    placed = (
        P(("groups", "expert"), None),
        P(("groups", "expert"), None),
        P(("groups", "expert"), None),
        P(("groups", "expert"), None),
        P("groups", None),
        P(("groups", "expert"), None, None),
        P(("groups", "expert"), None, None),
        P(("groups", "expert"), None, None),
    )
    return jax.shard_map(
        two_copies if mesh.shape["expert"] == 2 * PIECES else any_copies,
        mesh=mesh,
        in_specs=placed,
        out_specs=P(("groups", "expert"), None),
        check_vma=False,
    )
```

```python
import functools

import jax
import jax.numpy as jnp
from jax import lax
from jax.experimental import pallas as pl
from jax.experimental.pallas import tpu as pltpu
from jax.sharding import PartitionSpec as P

PIECES = 8
CAP = 12


def within(mib):
    return pltpu.CompilerParams(vmem_limit_bytes=mib * 2**20)


def expert_rows(arrived, gate_part, up_part, down_part):
    flattened = arrived.reshape(-1, arrived.shape[-1])
    gate_act = jnp.dot(flattened, gate_part, preferred_element_type=jnp.float32)
    up_act = jnp.dot(flattened, up_part, preferred_element_type=jnp.float32)
    hidden = (jax.nn.silu(gate_act) * up_act).astype(jnp.bfloat16)
    result = jnp.dot(hidden, down_part, preferred_element_type=jnp.float32).astype(jnp.bfloat16)
    return result.reshape(arrived.shape[:-1] + (down_part.shape[1],))


def any_copies(
    tokens, expert_ids, replica, gate_weights, slot_table, gate_pieces, up_pieces, down_pieces
):
    devices = lax.axis_size("expert")
    copies = devices // PIECES
    width = tokens.shape[1]
    specialist_extent = jnp.arange(slot_table.shape[0], dtype=jnp.int32)
    matches = (expert_ids[:, :, None] == specialist_extent[None, None, :]).astype(jnp.int32)
    per_replica = jnp.where(
        replica[:, :, None] == 0, slot_table[:, 0][None, None, :], slot_table[:, 1][None, None, :]
    )
    targets = jnp.sum(matches * per_replica, axis=2)
    copy_range = jnp.arange(copies, dtype=jnp.int32)
    members = (targets[:, :, None] == copy_range[None, None, :]).astype(jnp.int32)
    routed = jnp.sum(members, axis=1)
    position = jnp.cumsum(routed, axis=0) - routed
    retained = routed * (position < CAP).astype(jnp.int32)
    gate_copy = jnp.sum(gate_weights[:, :, None] * members.astype(jnp.float32), axis=1)
    slot_range = jnp.arange(CAP, dtype=jnp.int32)
    chosen_rows = retained.T[:, None, :] * (
        position.T[:, None, :] == slot_range[None, :, None]
    ).astype(jnp.int32)
    send_rows = jnp.einsum(
        "cjt,td->cjd", chosen_rows.astype(jnp.bfloat16), tokens, preferred_element_type=jnp.float32
    ).astype(jnp.bfloat16)
    gate_part = gate_pieces[0]
    up_part = up_pieces[0]
    down_part = down_pieces[0]
    outgoing = jnp.broadcast_to(send_rows[:, None], (copies, PIECES, CAP, width)).reshape(
        devices, CAP, width
    )
    arrived = lax.all_to_all(outgoing, "expert", split_axis=0, concat_axis=0, tiled=True)
    produced = expert_rows(arrived, gate_part, up_part, down_part)
    returned = lax.all_to_all(produced, "expert", split_axis=0, concat_axis=0, tiled=True)
    combined = jnp.sum(returned.reshape(copies, PIECES, CAP, width).astype(jnp.float32), axis=1)
    weighting = chosen_rows.astype(jnp.float32) * gate_copy.T[:, None, :]
    total = jnp.einsum("cjt,cjd->td", weighting, combined, precision=lax.Precision.HIGHEST)
    return total.astype(jnp.bfloat16)


def slots_of(ids, rep, table):
    experts = lax.broadcasted_iota(jnp.int32, table.shape, 1)
    here = table < 2
    first = jnp.sum(jnp.where(here, table, 0)[0:1], axis=1, keepdims=True)
    hosted = jnp.sum(jnp.where(here, experts, 0)[0:1], axis=1, keepdims=True)
    hit = ids == hosted
    copy = jnp.where(rep == 0, first, 1 - first)
    count = ids.shape[1]
    to = [jnp.sum(jnp.where(hit & (copy == c), 1.0, 0.0), axis=0, keepdims=True) for c in range(2)]
    earlier = (
        lax.broadcasted_iota(jnp.int32, (count, count), 0)
        < lax.broadcasted_iota(jnp.int32, (count, count), 1)
    ).astype(jnp.float32)
    slot = jnp.full((1, count), -1, jnp.int32)
    for c in range(2):
        routed = jnp.broadcast_to(to[c], (8, count))
        position = jnp.dot(routed, earlier, preferred_element_type=jnp.float32)[0:1]
        position = position.astype(jnp.int32)
        keep = (to[c] > 0.5) & (position < CAP)
        slot = jnp.where(keep, position + c * CAP, slot)
    return slot, hit


def copies_of(refs, sems):
    copies = [pltpu.make_async_copy(s, t, sems.at[i]) for i, (s, t) in enumerate(refs)]
    for copy in copies:
        copy.start()
    return copies


def pick_kernel(
    tok_hbm, ids_hbm, rep_hbm, table_hbm, w_hbm, out_ref, spread_ref,
    tok_ref, ids_ref, rep_ref, table_ref, w_ref, sems,
):
    copies = copies_of(
        [
            (ids_hbm, ids_ref),
            (rep_hbm, rep_ref),
            (table_hbm, table_ref),
            (w_hbm, w_ref),
            (tok_hbm, tok_ref),
        ],
        sems,
    )
    for copy in copies[:4]:
        copy.wait()
    slot, hit = slots_of(ids_ref[...], rep_ref[...], table_ref[...])
    weight = jnp.sum(jnp.where(hit, w_ref[...], 0.0), axis=0, keepdims=True)
    count = slot.shape[1]
    chosen = lax.broadcasted_iota(jnp.int32, (2 * CAP, count), 0) == slot
    spread_ref[...] = jnp.where(chosen, weight, 0.0)
    copies[4].wait()
    out_ref[...] = jnp.dot(
        chosen.astype(jnp.bfloat16), tok_ref[...], preferred_element_type=jnp.float32
    ).astype(jnp.bfloat16)


def activation(gate, up):
    return (gate / (1.0 + jnp.exp(-gate)) * up).astype(jnp.bfloat16)


def load_kernel(gate_hbm, up_hbm, down_hbm, gate_ref, up_ref, down_ref, sems):
    steps = sems.shape[1]
    pairs = []
    for source, target in ((gate_hbm, gate_ref), (up_hbm, up_ref), (down_hbm, down_ref)):
        step = source.shape[0] // steps
        for i in range(steps):
            part = pl.ds(i * step, step)
            pairs.append((source.at[part], target.at[part]))
    copies = [
        pltpu.make_async_copy(s, t, sems.at[i // steps, i % steps])
        for i, (s, t) in enumerate(pairs)
    ]
    for copy in copies:
        copy.start()
    for copy in copies:
        copy.wait()


def hold_kernel(*refs):
    pass


def expert_kernel(parts, *refs):
    gate_ref, up_ref, down_ref, mine_ref, other_ref, x_all = refs[-6:]
    rows = x_all.shape[0] // len(parts)
    for i, (which, block) in enumerate(parts):
        x_all[i * rows : (i + 1) * rows] = refs[which][block * rows : (block + 1) * rows]
    x = x_all[...]
    gate = jnp.dot(x, gate_ref[...], preferred_element_type=jnp.float32)
    up = jnp.dot(x, up_ref[...], preferred_element_type=jnp.float32)
    hidden = activation(gate, up)
    out = jnp.dot(hidden, down_ref[...], preferred_element_type=jnp.float32).astype(jnp.bfloat16)
    mine_ref[...] = out[: mine_ref.shape[0]]
    other_ref[...] = out[mine_ref.shape[0] :]


def add_kernel(mine_ref, passing_ref, out_ref):
    out_ref[...] = mine_ref[...].astype(jnp.float32) + passing_ref[...].astype(jnp.float32)


def settle_kernel(mine_ref, met_ref, side_ref, out_ref):
    rows = out_ref.shape[0]
    total = mine_ref[:rows].astype(jnp.float32) + met_ref[:rows].astype(jnp.float32)
    out_ref[...] = total + side_ref[...].astype(jnp.float32)


def combine_kernel(settled_ref, near_ref, spread_ref, out_ref):
    spread = spread_ref[...]
    spread_hi = spread.astype(jnp.bfloat16)
    spread_lo = (spread - spread_hi.astype(jnp.float32)).astype(jnp.bfloat16)
    dims = (((0,), (0,)), ((), ()))
    dot = functools.partial(
        lax.dot_general, dimension_numbers=dims, preferred_element_type=jnp.float32
    )
    total = settled_ref[...] + near_ref[...].astype(jnp.float32)
    total_hi = total.astype(jnp.bfloat16)
    total_lo = (total - total_hi.astype(jnp.float32)).astype(jnp.bfloat16)
    out = dot(spread_hi, total_hi) + (dot(spread_hi, total_lo) + dot(spread_lo, total_hi))
    out_ref[...] = out.astype(jnp.bfloat16)


def two_copies(
    tokens, expert_ids, replica, gate_weights, slot_table, gate_pieces, up_pieces, down_pieces
):
    devices = lax.axis_size("expert")
    count, width = tokens.shape
    rows = 2 * CAP
    hidden = gate_pieces.shape[2]
    bf16, f32 = jnp.bfloat16, jnp.float32
    in_hbm = pl.BlockSpec(memory_space=pltpu.HBM)
    in_vmem = pl.BlockSpec(memory_space=pltpu.VMEM)

    def partner(a):
        return lax.ppermute(a, "expert", [(i, i ^ 1) for i in range(devices)])

    def cross(a):
        return lax.ppermute(a, "expert", [(i, i ^ (4 if i % 2 else 2)) for i in range(devices)])

    def cross_back(a):
        return lax.ppermute(a, "expert", [(i, i ^ (2 if i % 2 else 4)) for i in range(devices)])

    def diagonal(a):
        return lax.ppermute(a, "expert", [(i, i ^ 6) for i in range(devices)])

    def add(a, b):
        return (a.astype(f32) + b.astype(f32)).astype(bf16)

    def cost(total):
        return pl.CostEstimate(
            flops=6 * total * width * hidden, bytes_accessed=6 * width * hidden, transcendentals=0
        )

    small = [expert_ids.T, replica.T, slot_table.T, gate_weights.T]
    own, spread = pl.pallas_call(
        pick_kernel,
        out_shape=[
            jax.ShapeDtypeStruct((rows, width), bf16),
            jax.ShapeDtypeStruct((rows, count), f32),
        ],
        in_specs=[in_hbm] * 5,
        scratch_shapes=[pltpu.VMEM(a.shape, a.dtype) for a in [tokens] + small]
        + [pltpu.SemaphoreType.DMA((5,))],
        compiler_params=within(56),
    )(tokens, *small)
    gate, up, down = pl.pallas_call(
        load_kernel,
        out_shape=[
            jax.ShapeDtypeStruct(a.shape[1:], bf16) for a in (gate_pieces, up_pieces, down_pieces)
        ],
        in_specs=[in_hbm] * 3,
        out_specs=[in_vmem] * 3,
        scratch_shapes=[pltpu.SemaphoreType.DMA((3, 8))],
        compiler_params=within(40),
        cost_estimate=cost(2 * rows),
    )(gate_pieces[0], up_pieces[0], down_pieces[0])

    def after(done, *arrays):
        anywhere = pl.BlockSpec(memory_space=pl.ANY)
        return pl.pallas_call(
            hold_kernel,
            out_shape=[jax.ShapeDtypeStruct(a.shape, a.dtype) for a in arrays],
            in_specs=[anywhere] * (1 + len(arrays)),
            out_specs=[anywhere] * len(arrays),
            input_output_aliases={1 + i: i for i in range(len(arrays))},
            compiler_params=within(1),
        )(done, *arrays)

    def early(array, micros):
        anywhere = pl.BlockSpec(memory_space=pl.ANY)
        return pl.pallas_call(
            hold_kernel,
            out_shape=jax.ShapeDtypeStruct(array.shape, array.dtype),
            in_specs=[anywhere],
            out_specs=anywhere,
            input_output_aliases={0: 0},
            compiler_params=within(1),
            cost_estimate=pl.CostEstimate(
                flops=micros * 10**9, bytes_accessed=0, transcendentals=0
            ),
        )(array)

    def experts(parts, *arrays):
        total = rows * len(parts)
        return pl.pallas_call(
            functools.partial(expert_kernel, parts),
            out_shape=[jax.ShapeDtypeStruct((total // 2, width), bf16)] * 2,
            scratch_shapes=[pltpu.VMEM((total, width), bf16)],
            compiler_params=within(24),
            cost_estimate=cost(total),
        )(*arrays, gate, up, down)

    twice = ((0, 0), (1, 0))
    near, = after(gate, cross(own))
    far = cross_back(near)
    side = cross_back(own)
    mine, other = experts(((0, 0), (1, 0), (2, 0), (3, 0)), own, near, partner(own), partner(near))
    met = partner(other)
    to_near = add(mine[rows:], met[rows:])
    far, = after(met, early(far, 10))
    got_near = early(cross(to_near), 10)
    far_mine, far_other = experts(twice, far, partner(far))
    to_far = add(far_mine, partner(far_other))
    settled = pl.pallas_call(
        settle_kernel,
        out_shape=jax.ShapeDtypeStruct((rows, width), f32),
        compiler_params=within(8),
    )(mine, met, got_near)
    to_far, = after(settled, to_far)
    passing = early(cross(to_far), 10)
    side = early(side, 10)
    side, side_1 = after(to_far, side, partner(side))
    side_mine, side_other = experts(twice, side, side_1)
    side_met = partner(side_other)
    part = pl.pallas_call(
        add_kernel,
        out_shape=jax.ShapeDtypeStruct((rows, width), f32),
        compiler_params=within(8),
    )(side_mine, passing)
    to_side = (part + side_met.astype(f32)).astype(bf16)
    got_side = cross_back(to_side)
    return pl.pallas_call(
        combine_kernel,
        out_shape=jax.ShapeDtypeStruct((count, width), bf16),
        compiler_params=within(24),
    )(settled, got_side, spread)


def solution(mesh):
    placed = (
        P(("groups", "expert"), None),
        P(("groups", "expert"), None),
        P(("groups", "expert"), None),
        P(("groups", "expert"), None),
        P("groups", None),
        P(("groups", "expert"), None, None),
        P(("groups", "expert"), None, None),
        P(("groups", "expert"), None, None),
    )
    return jax.shard_map(
        two_copies if mesh.shape["expert"] == 2 * PIECES else any_copies,
        mesh=mesh,
        in_specs=placed,
        out_specs=P(("groups", "expert"), None),
        check_vma=False,
    )
```

```python
import functools

import jax
import jax.numpy as jnp
from jax import lax
from jax.experimental import pallas as pl
from jax.experimental.pallas import tpu as pltpu
from jax.sharding import PartitionSpec as P

PIECES = 8
CAP = 12


def within(mib):
    return pltpu.CompilerParams(vmem_limit_bytes=mib * 2**20)


def expert_rows(arrived, gate_part, up_part, down_part):
    flattened = arrived.reshape(-1, arrived.shape[-1])
    gate_act = jnp.dot(flattened, gate_part, preferred_element_type=jnp.float32)
    up_act = jnp.dot(flattened, up_part, preferred_element_type=jnp.float32)
    hidden = (jax.nn.silu(gate_act) * up_act).astype(jnp.bfloat16)
    result = jnp.dot(hidden, down_part, preferred_element_type=jnp.float32).astype(jnp.bfloat16)
    return result.reshape(arrived.shape[:-1] + (down_part.shape[1],))


def any_copies(
    tokens, expert_ids, replica, gate_weights, slot_table, gate_pieces, up_pieces, down_pieces
):
    devices = lax.axis_size("expert")
    copies = devices // PIECES
    width = tokens.shape[1]
    specialist_extent = jnp.arange(slot_table.shape[0], dtype=jnp.int32)
    matches = (expert_ids[:, :, None] == specialist_extent[None, None, :]).astype(jnp.int32)
    per_replica = jnp.where(
        replica[:, :, None] == 0, slot_table[:, 0][None, None, :], slot_table[:, 1][None, None, :]
    )
    targets = jnp.sum(matches * per_replica, axis=2)
    copy_range = jnp.arange(copies, dtype=jnp.int32)
    members = (targets[:, :, None] == copy_range[None, None, :]).astype(jnp.int32)
    routed = jnp.sum(members, axis=1)
    position = jnp.cumsum(routed, axis=0) - routed
    retained = routed * (position < CAP).astype(jnp.int32)
    gate_copy = jnp.sum(gate_weights[:, :, None] * members.astype(jnp.float32), axis=1)
    slot_range = jnp.arange(CAP, dtype=jnp.int32)
    chosen_rows = retained.T[:, None, :] * (
        position.T[:, None, :] == slot_range[None, :, None]
    ).astype(jnp.int32)
    send_rows = jnp.einsum(
        "cjt,td->cjd", chosen_rows.astype(jnp.bfloat16), tokens, preferred_element_type=jnp.float32
    ).astype(jnp.bfloat16)
    gate_part = gate_pieces[0]
    up_part = up_pieces[0]
    down_part = down_pieces[0]
    outgoing = jnp.broadcast_to(send_rows[:, None], (copies, PIECES, CAP, width)).reshape(
        devices, CAP, width
    )
    arrived = lax.all_to_all(outgoing, "expert", split_axis=0, concat_axis=0, tiled=True)
    produced = expert_rows(arrived, gate_part, up_part, down_part)
    returned = lax.all_to_all(produced, "expert", split_axis=0, concat_axis=0, tiled=True)
    combined = jnp.sum(returned.reshape(copies, PIECES, CAP, width).astype(jnp.float32), axis=1)
    weighting = chosen_rows.astype(jnp.float32) * gate_copy.T[:, None, :]
    total = jnp.einsum("cjt,cjd->td", weighting, combined, precision=lax.Precision.HIGHEST)
    return total.astype(jnp.bfloat16)


def slots_of(ids, rep, table):
    experts = lax.broadcasted_iota(jnp.int32, table.shape, 1)
    here = table < 2
    first = jnp.sum(jnp.where(here, table, 0)[0:1], axis=1, keepdims=True)
    hosted = jnp.sum(jnp.where(here, experts, 0)[0:1], axis=1, keepdims=True)
    hit = ids == hosted
    copy = jnp.where(rep == 0, first, 1 - first)
    count = ids.shape[1]
    to = [jnp.sum(jnp.where(hit & (copy == c), 1.0, 0.0), axis=0, keepdims=True) for c in range(2)]
    earlier = (
        lax.broadcasted_iota(jnp.int32, (count, count), 0)
        < lax.broadcasted_iota(jnp.int32, (count, count), 1)
    ).astype(jnp.float32)
    slot = jnp.full((1, count), -1, jnp.int32)
    for c in range(2):
        routed = jnp.broadcast_to(to[c], (8, count))
        position = jnp.dot(routed, earlier, preferred_element_type=jnp.float32)[0:1]
        position = position.astype(jnp.int32)
        keep = (to[c] > 0.5) & (position < CAP)
        slot = jnp.where(keep, position + c * CAP, slot)
    return slot, hit


def copies_of(refs, sems):
    copies = [pltpu.make_async_copy(s, t, sems.at[i]) for i, (s, t) in enumerate(refs)]
    for copy in copies:
        copy.start()
    return copies


def pick_kernel(
    tok_hbm, ids_hbm, rep_hbm, table_hbm, w_hbm, out_ref, spread_ref,
    tok_ref, ids_ref, rep_ref, table_ref, w_ref, sems,
):
    copies = copies_of(
        [
            (ids_hbm, ids_ref),
            (rep_hbm, rep_ref),
            (table_hbm, table_ref),
            (w_hbm, w_ref),
            (tok_hbm, tok_ref),
        ],
        sems,
    )
    for copy in copies[:4]:
        copy.wait()
    slot, hit = slots_of(ids_ref[...], rep_ref[...], table_ref[...])
    weight = jnp.sum(jnp.where(hit, w_ref[...], 0.0), axis=0, keepdims=True)
    count = slot.shape[1]
    chosen = lax.broadcasted_iota(jnp.int32, (2 * CAP, count), 0) == slot
    spread_ref[...] = jnp.where(chosen, weight, 0.0)
    copies[4].wait()
    out_ref[...] = jnp.dot(
        chosen.astype(jnp.bfloat16), tok_ref[...], preferred_element_type=jnp.float32
    ).astype(jnp.bfloat16)


def activation(gate, up):
    return (gate / (1.0 + jnp.exp(-gate)) * up).astype(jnp.bfloat16)


def load_kernel(gate_hbm, up_hbm, down_hbm, gate_ref, up_ref, down_ref, sems):
    steps = sems.shape[1]
    pairs = []
    for source, target in ((gate_hbm, gate_ref), (up_hbm, up_ref), (down_hbm, down_ref)):
        step = source.shape[0] // steps
        for i in range(steps):
            part = pl.ds(i * step, step)
            pairs.append((source.at[part], target.at[part]))
    copies = [
        pltpu.make_async_copy(s, t, sems.at[i // steps, i % steps])
        for i, (s, t) in enumerate(pairs)
    ]
    for copy in copies:
        copy.start()
    for copy in copies:
        copy.wait()


def hold_kernel(*refs):
    pass


def expert_kernel(parts, *refs):
    gate_ref, up_ref, down_ref, mine_ref, other_ref, x_all = refs[-6:]
    rows = x_all.shape[0] // len(parts)
    for i, (which, block) in enumerate(parts):
        x_all[i * rows : (i + 1) * rows] = refs[which][block * rows : (block + 1) * rows]
    x = x_all[...]
    gate = jnp.dot(x, gate_ref[...], preferred_element_type=jnp.float32)
    up = jnp.dot(x, up_ref[...], preferred_element_type=jnp.float32)
    hidden = activation(gate, up)
    out = jnp.dot(hidden, down_ref[...], preferred_element_type=jnp.float32).astype(jnp.bfloat16)
    mine_ref[...] = out[: mine_ref.shape[0]]
    other_ref[...] = out[mine_ref.shape[0] :]


def add_kernel(mine_ref, passing_ref, out_ref):
    out_ref[...] = mine_ref[...].astype(jnp.float32) + passing_ref[...].astype(jnp.float32)


def settle_kernel(mine_ref, met_ref, side_ref, out_ref):
    rows = out_ref.shape[0]
    total = mine_ref[:rows].astype(jnp.float32) + met_ref[:rows].astype(jnp.float32)
    out_ref[...] = total + side_ref[...].astype(jnp.float32)


def combine_kernel(settled_ref, near_ref, spread_ref, out_ref):
    spread = spread_ref[...]
    spread_hi = spread.astype(jnp.bfloat16)
    spread_lo = (spread - spread_hi.astype(jnp.float32)).astype(jnp.bfloat16)
    dims = (((0,), (0,)), ((), ()))
    dot = functools.partial(
        lax.dot_general, dimension_numbers=dims, preferred_element_type=jnp.float32
    )
    total = settled_ref[...] + near_ref[...].astype(jnp.float32)
    total_hi = total.astype(jnp.bfloat16)
    total_lo = (total - total_hi.astype(jnp.float32)).astype(jnp.bfloat16)
    out = dot(spread_hi, total_hi) + (dot(spread_hi, total_lo) + dot(spread_lo, total_hi))
    out_ref[...] = out.astype(jnp.bfloat16)


def two_copies(
    tokens, expert_ids, replica, gate_weights, slot_table, gate_pieces, up_pieces, down_pieces
):
    devices = lax.axis_size("expert")
    count, width = tokens.shape
    rows = 2 * CAP
    hidden = gate_pieces.shape[2]
    bf16, f32 = jnp.bfloat16, jnp.float32
    in_hbm = pl.BlockSpec(memory_space=pltpu.HBM)
    in_vmem = pl.BlockSpec(memory_space=pltpu.VMEM)

    def partner(a):
        return lax.ppermute(a, "expert", [(i, i ^ 1) for i in range(devices)])

    def cross(a):
        return lax.ppermute(a, "expert", [(i, i ^ (4 if i % 2 else 2)) for i in range(devices)])

    def cross_back(a):
        return lax.ppermute(a, "expert", [(i, i ^ (2 if i % 2 else 4)) for i in range(devices)])

    def diagonal(a):
        return lax.ppermute(a, "expert", [(i, i ^ 6) for i in range(devices)])

    def add(a, b):
        return (a.astype(f32) + b.astype(f32)).astype(bf16)

    def cost(total):
        return pl.CostEstimate(
            flops=6 * total * width * hidden, bytes_accessed=6 * width * hidden, transcendentals=0
        )

    small = [expert_ids.T, replica.T, slot_table.T, gate_weights.T]
    own, spread = pl.pallas_call(
        pick_kernel,
        out_shape=[
            jax.ShapeDtypeStruct((rows, width), bf16),
            jax.ShapeDtypeStruct((rows, count), f32),
        ],
        in_specs=[in_hbm] * 5,
        scratch_shapes=[pltpu.VMEM(a.shape, a.dtype) for a in [tokens] + small]
        + [pltpu.SemaphoreType.DMA((5,))],
        compiler_params=within(56),
    )(tokens, *small)
    gate, up, down = pl.pallas_call(
        load_kernel,
        out_shape=[
            jax.ShapeDtypeStruct(a.shape[1:], bf16) for a in (gate_pieces, up_pieces, down_pieces)
        ],
        in_specs=[in_hbm] * 3,
        out_specs=[in_vmem] * 3,
        scratch_shapes=[pltpu.SemaphoreType.DMA((3, 8))],
        compiler_params=within(40),
        cost_estimate=cost(2 * rows),
    )(gate_pieces[0], up_pieces[0], down_pieces[0])

    def after(done, *arrays):
        anywhere = pl.BlockSpec(memory_space=pl.ANY)
        return pl.pallas_call(
            hold_kernel,
            out_shape=[jax.ShapeDtypeStruct(a.shape, a.dtype) for a in arrays],
            in_specs=[anywhere] * (1 + len(arrays)),
            out_specs=[anywhere] * len(arrays),
            input_output_aliases={1 + i: i for i in range(len(arrays))},
            compiler_params=within(1),
        )(done, *arrays)

    def early(array, micros):
        anywhere = pl.BlockSpec(memory_space=pl.ANY)
        return pl.pallas_call(
            hold_kernel,
            out_shape=jax.ShapeDtypeStruct(array.shape, array.dtype),
            in_specs=[anywhere],
            out_specs=anywhere,
            input_output_aliases={0: 0},
            compiler_params=within(1),
            cost_estimate=pl.CostEstimate(
                flops=micros * 10**9, bytes_accessed=0, transcendentals=0
            ),
        )(array)

    def experts(parts, *arrays):
        total = rows * len(parts)
        return pl.pallas_call(
            functools.partial(expert_kernel, parts),
            out_shape=[jax.ShapeDtypeStruct((total // 2, width), bf16)] * 2,
            scratch_shapes=[pltpu.VMEM((total, width), bf16)],
            compiler_params=within(24),
            cost_estimate=cost(total),
        )(*arrays, gate, up, down)

    twice = ((0, 0), (1, 0))
    near, = after(gate, cross(own))
    far = cross_back(near)
    side = cross_back(own)
    mine, other = experts(((0, 0), (1, 0), (2, 0), (3, 0)), own, near, partner(own), partner(near))
    met = partner(other)
    to_near = add(mine[rows:], met[rows:])
    far, = after(met, early(far, 10))
    far_mine, far_other = experts(twice, far, partner(far))
    to_far = add(far_mine, partner(far_other))
    passing = early(cross(to_far), 10)
    got_near = cross(to_near)
    side, side_1 = after(to_far, side, partner(side))
    side_mine, side_other = experts(twice, side, side_1)
    side_met = partner(side_other)
    part = pl.pallas_call(
        add_kernel,
        out_shape=jax.ShapeDtypeStruct((rows, width), f32),
        compiler_params=within(8),
    )(side_mine, passing)
    to_side = (part + side_met.astype(f32)).astype(bf16)
    got_near, = after(side_mine, got_near)
    settled = pl.pallas_call(
        settle_kernel,
        out_shape=jax.ShapeDtypeStruct((rows, width), f32),
        compiler_params=within(8),
    )(mine, met, got_near)
    got_side = cross_back(to_side)
    return pl.pallas_call(
        combine_kernel,
        out_shape=jax.ShapeDtypeStruct((count, width), bf16),
        compiler_params=within(24),
    )(settled, got_side, spread)


def solution(mesh):
    placed = (
        P(("groups", "expert"), None),
        P(("groups", "expert"), None),
        P(("groups", "expert"), None),
        P(("groups", "expert"), None),
        P("groups", None),
        P(("groups", "expert"), None, None),
        P(("groups", "expert"), None, None),
        P(("groups", "expert"), None, None),
    )
    return jax.shard_map(
        two_copies if mesh.shape["expert"] == 2 * PIECES else any_copies,
        mesh=mesh,
        in_specs=placed,
        out_specs=P(("groups", "expert"), None),
        check_vma=False,
    )
```

```python
import functools

import jax
import jax.numpy as jnp
from jax import lax
from jax.experimental import pallas as pl
from jax.experimental.pallas import tpu as pltpu
from jax.sharding import PartitionSpec as P

PIECES = 8
CAP = 12


def within(mib):
    return pltpu.CompilerParams(vmem_limit_bytes=mib * 2**20)


def expert_rows(arrived, gate_part, up_part, down_part):
    flattened = arrived.reshape(-1, arrived.shape[-1])
    gate_act = jnp.dot(flattened, gate_part, preferred_element_type=jnp.float32)
    up_act = jnp.dot(flattened, up_part, preferred_element_type=jnp.float32)
    hidden = (jax.nn.silu(gate_act) * up_act).astype(jnp.bfloat16)
    result = jnp.dot(hidden, down_part, preferred_element_type=jnp.float32).astype(jnp.bfloat16)
    return result.reshape(arrived.shape[:-1] + (down_part.shape[1],))


def any_copies(
    tokens, expert_ids, replica, gate_weights, slot_table, gate_pieces, up_pieces, down_pieces
):
    devices = lax.axis_size("expert")
    copies = devices // PIECES
    width = tokens.shape[1]
    specialist_extent = jnp.arange(slot_table.shape[0], dtype=jnp.int32)
    matches = (expert_ids[:, :, None] == specialist_extent[None, None, :]).astype(jnp.int32)
    per_replica = jnp.where(
        replica[:, :, None] == 0, slot_table[:, 0][None, None, :], slot_table[:, 1][None, None, :]
    )
    targets = jnp.sum(matches * per_replica, axis=2)
    copy_range = jnp.arange(copies, dtype=jnp.int32)
    members = (targets[:, :, None] == copy_range[None, None, :]).astype(jnp.int32)
    routed = jnp.sum(members, axis=1)
    position = jnp.cumsum(routed, axis=0) - routed
    retained = routed * (position < CAP).astype(jnp.int32)
    gate_copy = jnp.sum(gate_weights[:, :, None] * members.astype(jnp.float32), axis=1)
    slot_range = jnp.arange(CAP, dtype=jnp.int32)
    chosen_rows = retained.T[:, None, :] * (
        position.T[:, None, :] == slot_range[None, :, None]
    ).astype(jnp.int32)
    send_rows = jnp.einsum(
        "cjt,td->cjd", chosen_rows.astype(jnp.bfloat16), tokens, preferred_element_type=jnp.float32
    ).astype(jnp.bfloat16)
    gate_part = gate_pieces[0]
    up_part = up_pieces[0]
    down_part = down_pieces[0]
    outgoing = jnp.broadcast_to(send_rows[:, None], (copies, PIECES, CAP, width)).reshape(
        devices, CAP, width
    )
    arrived = lax.all_to_all(outgoing, "expert", split_axis=0, concat_axis=0, tiled=True)
    produced = expert_rows(arrived, gate_part, up_part, down_part)
    returned = lax.all_to_all(produced, "expert", split_axis=0, concat_axis=0, tiled=True)
    combined = jnp.sum(returned.reshape(copies, PIECES, CAP, width).astype(jnp.float32), axis=1)
    weighting = chosen_rows.astype(jnp.float32) * gate_copy.T[:, None, :]
    total = jnp.einsum("cjt,cjd->td", weighting, combined, precision=lax.Precision.HIGHEST)
    return total.astype(jnp.bfloat16)


def slots_of(ids, rep, table):
    experts = lax.broadcasted_iota(jnp.int32, table.shape, 1)
    here = table < 2
    first = jnp.sum(jnp.where(here, table, 0)[0:1], axis=1, keepdims=True)
    hosted = jnp.sum(jnp.where(here, experts, 0)[0:1], axis=1, keepdims=True)
    hit = ids == hosted
    copy = jnp.where(rep == 0, first, 1 - first)
    count = ids.shape[1]
    some = jnp.sum(jnp.where(hit, 1, 0), axis=0, keepdims=True)
    copy = jnp.sum(jnp.where(hit, copy, 0), axis=0, keepdims=True)
    lanes = lax.broadcasted_iota(jnp.int32, (8, count), 0)
    routed = ((lanes == copy) & (some > 0)).astype(jnp.float32)
    earlier = (
        lax.broadcasted_iota(jnp.int32, (count, count), 0)
        < lax.broadcasted_iota(jnp.int32, (count, count), 1)
    ).astype(jnp.float32)
    position = jnp.dot(routed, earlier, preferred_element_type=jnp.float32)
    position = jnp.sum(routed * position, axis=0, keepdims=True).astype(jnp.int32)
    slot = jnp.where((some > 0) & (position < CAP), position + copy * CAP, -1)
    return slot, hit


def copies_of(refs, sems):
    copies = [pltpu.make_async_copy(s, t, sems.at[i]) for i, (s, t) in enumerate(refs)]
    for copy in copies:
        copy.start()
    return copies


def pick_kernel(
    tok_hbm, ids_hbm, rep_hbm, table_hbm, w_hbm, out_ref, chosen_ref, weight_ref,
    tok_ref, ids_ref, rep_ref, table_ref, w_ref, sems,
):
    copies = copies_of(
        [
            (ids_hbm, ids_ref),
            (rep_hbm, rep_ref),
            (table_hbm, table_ref),
            (w_hbm, w_ref),
            (tok_hbm, tok_ref),
        ],
        sems,
    )
    for copy in copies[:4]:
        copy.wait()
    slot, hit = slots_of(ids_ref[...], rep_ref[...], table_ref[...])
    count = slot.shape[1]
    chosen = lax.broadcasted_iota(jnp.int32, (2 * CAP, count), 0) == slot
    chosen = chosen.astype(jnp.bfloat16)
    copies[4].wait()
    out_ref[...] = jnp.dot(
        chosen, tok_ref[...], preferred_element_type=jnp.float32
    ).astype(jnp.bfloat16)
    chosen_ref[...] = chosen
    weight = jnp.sum(jnp.where(hit, w_ref[...], 0.0), axis=0, keepdims=True)
    square = [lax.broadcasted_iota(jnp.int32, (count, count), i) for i in range(2)]
    diagonal = jnp.where(square[0] == square[1], weight, 0.0)
    weight_ref[...] = jnp.sum(diagonal, axis=1, keepdims=True)


def activation(gate, up):
    return (gate / (1.0 + jnp.exp(-gate)) * up).astype(jnp.bfloat16)


def load_kernel(_, gate_hbm, up_hbm, down_hbm, gate_ref, up_ref, down_ref, sems):
    steps = sems.shape[1]
    pairs = []
    for source, target in ((gate_hbm, gate_ref), (up_hbm, up_ref), (down_hbm, down_ref)):
        step = source.shape[0] // steps
        for i in range(steps):
            part = pl.ds(i * step, step)
            pairs.append((source.at[part], target.at[part]))
    copies = [
        pltpu.make_async_copy(s, t, sems.at[i // steps, i % steps])
        for i, (s, t) in enumerate(pairs)
    ]
    for copy in copies:
        copy.start()
    for copy in copies:
        copy.wait()


def hold_kernel(*refs):
    pass


def expert_kernel(*refs):
    gate_ref, up_ref, down_ref, mine_ref, other_ref, x_all = refs[-6:]
    rows = refs[0].shape[0]
    for i, ref in enumerate(refs[:-6]):
        x_all[i * rows : (i + 1) * rows] = ref[...]
    for i in range(len(refs) - 6, x_all.shape[0] // rows):
        x_all[i * rows : (i + 1) * rows] = refs[0][...]
    x = x_all[...]
    gate = jnp.dot(x, gate_ref[...], preferred_element_type=jnp.float32)
    up = jnp.dot(x, up_ref[...], preferred_element_type=jnp.float32)
    hidden = activation(gate, up)
    out = jnp.dot(hidden, down_ref[...], preferred_element_type=jnp.float32).astype(jnp.bfloat16)
    mine_ref[...] = out[: mine_ref.shape[0]]
    other_ref[...] = out[mine_ref.shape[0] : mine_ref.shape[0] + other_ref.shape[0]]


def side_kernel(mine_ref, met_ref, _, out_ref):
    rows = out_ref.shape[0]
    out_ref[...] = mine_ref[rows:].astype(jnp.float32) + met_ref[2 * rows :].astype(jnp.float32)


def settle_kernel(mine_ref, met_ref, side_ref, out_ref):
    rows = out_ref.shape[0]
    total = mine_ref[:rows].astype(jnp.float32) + met_ref[:rows].astype(jnp.float32)
    out_ref[...] = total + side_ref[...].astype(jnp.float32)


def combine_kernel(settled_ref, side_ref, chosen_ref, weight_ref, out_hbm, out_ref, sems):
    chosen, weight = chosen_ref[...], weight_ref[...]
    steps = sems.shape[0]
    step = out_ref.shape[1] // steps
    copies = []
    for i in range(steps):
        part = slice(i * step, (i + 1) * step)
        total = settled_ref[:, part] + side_ref[:, part].astype(jnp.float32)
        out = lax.dot_general(
            chosen, total.astype(jnp.bfloat16), (((0,), (0,)), ((), ())),
            preferred_element_type=jnp.float32,
        )
        out_ref[:, part] = (weight * out).astype(jnp.bfloat16)
        copies.append(pltpu.make_async_copy(out_ref.at[:, part], out_hbm.at[:, part], sems.at[i]))
        copies[-1].start()
    for copy in copies:
        copy.wait()


def two_copies(
    tokens, expert_ids, replica, gate_weights, slot_table, gate_pieces, up_pieces, down_pieces
):
    devices = lax.axis_size("expert")
    count, width = tokens.shape
    rows = 2 * CAP
    hidden = gate_pieces.shape[2]
    bf16, f32 = jnp.bfloat16, jnp.float32
    in_hbm = pl.BlockSpec(memory_space=pltpu.HBM)
    in_vmem = pl.BlockSpec(memory_space=pltpu.VMEM)

    def partner(a):
        return lax.ppermute(a, "expert", [(i, i ^ 1) for i in range(devices)])

    def cross(a):
        return lax.ppermute(a, "expert", [(i, i ^ (4 if i % 2 else 2)) for i in range(devices)])

    def cross_back(a):
        return lax.ppermute(a, "expert", [(i, i ^ (2 if i % 2 else 4)) for i in range(devices)])

    def diagonal(a):
        return lax.ppermute(a, "expert", [(i, i ^ 6) for i in range(devices)])

    def add(a, b):
        return (a.astype(f32) + b.astype(f32)).astype(bf16)

    def cost(total):
        return pl.CostEstimate(
            flops=6 * total * width * hidden, bytes_accessed=6 * width * hidden, transcendentals=0
        )

    small = [expert_ids.T, replica.T, slot_table.T, gate_weights.T]
    own, chosen, weight = pl.pallas_call(
        pick_kernel,
        out_shape=[
            jax.ShapeDtypeStruct((rows, width), bf16),
            jax.ShapeDtypeStruct((rows, count), bf16),
            jax.ShapeDtypeStruct((count, 1), f32),
        ],
        in_specs=[in_hbm] * 5,
        scratch_shapes=[pltpu.VMEM(a.shape, a.dtype) for a in [tokens] + small]
        + [pltpu.SemaphoreType.DMA((5,))],
        compiler_params=within(56),
    )(tokens, *small)
    own_1 = partner(own)
    gate, up, down = pl.pallas_call(
        load_kernel,
        out_shape=[
            jax.ShapeDtypeStruct(a.shape[1:], bf16) for a in (gate_pieces, up_pieces, down_pieces)
        ],
        in_specs=[pl.BlockSpec(memory_space=pl.ANY)] + [in_hbm] * 3,
        out_specs=[in_vmem] * 3,
        scratch_shapes=[pltpu.SemaphoreType.DMA((3, 8))],
        compiler_params=within(40),
        cost_estimate=cost(2 * rows),
    )(own_1, gate_pieces[0], up_pieces[0], down_pieces[0])

    def after(done, *arrays):
        anywhere = pl.BlockSpec(memory_space=pl.ANY)
        return pl.pallas_call(
            hold_kernel,
            out_shape=[jax.ShapeDtypeStruct(a.shape, a.dtype) for a in arrays],
            in_specs=[anywhere] * (1 + len(arrays)),
            out_specs=[anywhere] * len(arrays),
            input_output_aliases={1 + i: i for i in range(len(arrays))},
            compiler_params=within(1),
        )(done, *arrays)

    def early(array, micros):
        anywhere = pl.BlockSpec(memory_space=pl.ANY)
        return pl.pallas_call(
            hold_kernel,
            out_shape=jax.ShapeDtypeStruct(array.shape, array.dtype),
            in_specs=[anywhere],
            out_specs=anywhere,
            input_output_aliases={0: 0},
            compiler_params=within(1),
            cost_estimate=pl.CostEstimate(
                flops=micros * 10**9, bytes_accessed=0, transcendentals=0
            ),
        )(array)

    def experts(blocks, mine, *arrays):
        total = rows * blocks
        return pl.pallas_call(
            expert_kernel,
            out_shape=[
                jax.ShapeDtypeStruct((rows * mine, width), bf16),
                jax.ShapeDtypeStruct((rows * (blocks - mine), width), bf16),
            ],
            scratch_shapes=[pltpu.VMEM((max(total, 5 * rows), width), bf16)],
            compiler_params=within(24),
            cost_estimate=cost(total),
        )(*arrays, gate, up, down)

    near, = after(gate, cross(own))
    side_1, = after(gate, cross(own_1))
    far = cross_back(near)
    mine, other = experts(5, 2, own, near, own_1, partner(near), side_1)
    met = partner(other)
    block = [slice(i * rows, (i + 1) * rows) for i in range(3)]
    to_near = add(mine[block[1]], met[block[1]])
    side = partner(side_1)
    far, = after(met, early(far, 10))
    last_mine, last_other = experts(3, 2, far, side, partner(far))
    to_far = add(last_mine[:rows], partner(last_other))
    passing = early(cross(to_far), 10)
    to_side = pl.pallas_call(
        side_kernel,
        out_shape=jax.ShapeDtypeStruct((rows, width), f32),
        in_specs=[in_vmem] * 2 + [pl.BlockSpec(memory_space=pl.ANY)],
        compiler_params=within(8),
        cost_estimate=cost(10 * rows),
    )(last_mine, met, to_far)
    got_side = cross_back((to_side + passing.astype(f32)).astype(bf16))
    got_near, = after(to_side, cross(to_near))
    settled = pl.pallas_call(
        settle_kernel,
        out_shape=jax.ShapeDtypeStruct((rows, width), f32),
        compiler_params=within(8),
    )(mine, met, got_near)
    return pl.pallas_call(
        combine_kernel,
        out_shape=jax.ShapeDtypeStruct((count, width), bf16),
        out_specs=pl.BlockSpec(memory_space=pl.ANY),
        scratch_shapes=[pltpu.VMEM((count, width), bf16), pltpu.SemaphoreType.DMA((4,))],
        compiler_params=within(24),
    )(settled, got_side, chosen, weight)


def solution(mesh):
    placed = (
        P(("groups", "expert"), None),
        P(("groups", "expert"), None),
        P(("groups", "expert"), None),
        P(("groups", "expert"), None),
        P("groups", None),
        P(("groups", "expert"), None, None),
        P(("groups", "expert"), None, None),
        P(("groups", "expert"), None, None),
    )
    return jax.shard_map(
        two_copies if mesh.shape["expert"] == 2 * PIECES else any_copies,
        mesh=mesh,
        in_specs=placed,
        out_specs=P(("groups", "expert"), None),
        check_vma=False,
    )
```

```python
import functools

import jax
import jax.numpy as jnp
from jax import lax
from jax.experimental import pallas as pl
from jax.experimental.pallas import tpu as pltpu
from jax.sharding import PartitionSpec as P

PIECES = 8
CAP = 12


def within(mib):
    return pltpu.CompilerParams(vmem_limit_bytes=mib * 2**20)


def expert_rows(arrived, gate_part, up_part, down_part):
    flattened = arrived.reshape(-1, arrived.shape[-1])
    gate_act = jnp.dot(flattened, gate_part, preferred_element_type=jnp.float32)
    up_act = jnp.dot(flattened, up_part, preferred_element_type=jnp.float32)
    hidden = (jax.nn.silu(gate_act) * up_act).astype(jnp.bfloat16)
    result = jnp.dot(hidden, down_part, preferred_element_type=jnp.float32).astype(jnp.bfloat16)
    return result.reshape(arrived.shape[:-1] + (down_part.shape[1],))


def any_copies(
    tokens, expert_ids, replica, gate_weights, slot_table, gate_pieces, up_pieces, down_pieces
):
    devices = lax.axis_size("expert")
    copies = devices // PIECES
    width = tokens.shape[1]
    specialist_extent = jnp.arange(slot_table.shape[0], dtype=jnp.int32)
    matches = (expert_ids[:, :, None] == specialist_extent[None, None, :]).astype(jnp.int32)
    per_replica = jnp.where(
        replica[:, :, None] == 0, slot_table[:, 0][None, None, :], slot_table[:, 1][None, None, :]
    )
    targets = jnp.sum(matches * per_replica, axis=2)
    copy_range = jnp.arange(copies, dtype=jnp.int32)
    members = (targets[:, :, None] == copy_range[None, None, :]).astype(jnp.int32)
    routed = jnp.sum(members, axis=1)
    position = jnp.cumsum(routed, axis=0) - routed
    retained = routed * (position < CAP).astype(jnp.int32)
    gate_copy = jnp.sum(gate_weights[:, :, None] * members.astype(jnp.float32), axis=1)
    slot_range = jnp.arange(CAP, dtype=jnp.int32)
    chosen_rows = retained.T[:, None, :] * (
        position.T[:, None, :] == slot_range[None, :, None]
    ).astype(jnp.int32)
    send_rows = jnp.einsum(
        "cjt,td->cjd", chosen_rows.astype(jnp.bfloat16), tokens, preferred_element_type=jnp.float32
    ).astype(jnp.bfloat16)
    gate_part = gate_pieces[0]
    up_part = up_pieces[0]
    down_part = down_pieces[0]
    outgoing = jnp.broadcast_to(send_rows[:, None], (copies, PIECES, CAP, width)).reshape(
        devices, CAP, width
    )
    arrived = lax.all_to_all(outgoing, "expert", split_axis=0, concat_axis=0, tiled=True)
    produced = expert_rows(arrived, gate_part, up_part, down_part)
    returned = lax.all_to_all(produced, "expert", split_axis=0, concat_axis=0, tiled=True)
    combined = jnp.sum(returned.reshape(copies, PIECES, CAP, width).astype(jnp.float32), axis=1)
    weighting = chosen_rows.astype(jnp.float32) * gate_copy.T[:, None, :]
    total = jnp.einsum("cjt,cjd->td", weighting, combined, precision=lax.Precision.HIGHEST)
    return total.astype(jnp.bfloat16)


def slots_of(ids, rep, table):
    experts = lax.broadcasted_iota(jnp.int32, table.shape, 1)
    here = table < 2
    first = jnp.sum(jnp.where(here, table, 0)[0:1], axis=1, keepdims=True)
    hosted = jnp.sum(jnp.where(here, experts, 0)[0:1], axis=1, keepdims=True)
    hit = ids == hosted
    copy = jnp.where(rep == 0, first, 1 - first)
    count = ids.shape[1]
    some = jnp.sum(jnp.where(hit, 1, 0), axis=0, keepdims=True)
    copy = jnp.sum(jnp.where(hit, copy, 0), axis=0, keepdims=True)
    lanes = lax.broadcasted_iota(jnp.int32, (8, count), 0)
    routed = ((lanes == copy) & (some > 0)).astype(jnp.float32)
    earlier = (
        lax.broadcasted_iota(jnp.int32, (count, count), 0)
        < lax.broadcasted_iota(jnp.int32, (count, count), 1)
    ).astype(jnp.float32)
    position = jnp.dot(routed, earlier, preferred_element_type=jnp.float32)
    position = jnp.sum(routed * position, axis=0, keepdims=True).astype(jnp.int32)
    slot = jnp.where((some > 0) & (position < CAP), position + copy * CAP, -1)
    return slot, hit


def copies_of(refs, sems):
    copies = [pltpu.make_async_copy(s, t, sems.at[i]) for i, (s, t) in enumerate(refs)]
    for copy in copies:
        copy.start()
    return copies


def pick_kernel(
    tok_hbm, ids_hbm, rep_hbm, table_hbm, w_hbm, out_ref, chosen_ref, weight_ref,
    tok_ref, ids_ref, rep_ref, table_ref, w_ref, sems,
):
    copies = copies_of(
        [
            (ids_hbm, ids_ref),
            (rep_hbm, rep_ref),
            (table_hbm, table_ref),
            (w_hbm, w_ref),
            (tok_hbm, tok_ref),
        ],
        sems,
    )
    for copy in copies[:4]:
        copy.wait()
    slot, hit = slots_of(ids_ref[...], rep_ref[...], table_ref[...])
    count = slot.shape[1]
    chosen = lax.broadcasted_iota(jnp.int32, (2 * CAP, count), 0) == slot
    chosen = chosen.astype(jnp.bfloat16)
    copies[4].wait()
    out_ref[...] = jnp.dot(
        chosen, tok_ref[...], preferred_element_type=jnp.float32
    ).astype(jnp.bfloat16)
    chosen_ref[...] = chosen
    weight = jnp.sum(jnp.where(hit, w_ref[...], 0.0), axis=0, keepdims=True)
    square = [lax.broadcasted_iota(jnp.int32, (count, count), i) for i in range(2)]
    diagonal = jnp.where(square[0] == square[1], weight, 0.0)
    weight_ref[...] = jnp.sum(diagonal, axis=1, keepdims=True)


def activation(gate, up):
    return (gate / (1.0 + jnp.exp(-gate)) * up).astype(jnp.bfloat16)


def load_kernel(*refs):
    refs, sems = refs[1:-1], refs[-1]
    count, steps = sems.shape
    pairs = []
    for source, target in zip(refs[:count], refs[count:]):
        step = source.shape[0] // steps
        for i in range(steps):
            part = pl.ds(i * step, step)
            pairs.append((source.at[part], target.at[part]))
    copies = [
        pltpu.make_async_copy(s, t, sems.at[i // steps, i % steps])
        for i, (s, t) in enumerate(pairs)
    ]
    for copy in copies:
        copy.start()
    for copy in copies:
        copy.wait()


def hold_kernel(*refs):
    pass


def expert_kernel(blocks, *refs):
    gate_ref, up_ref, down_ref = refs[blocks : blocks + 3]
    out_refs, x_all = refs[blocks + 3 : -1], refs[-1]
    rows = refs[0].shape[0]
    for i in range(blocks):
        x_all[i * rows : (i + 1) * rows] = refs[i][...]
    for i in range(blocks, x_all.shape[0] // rows):
        x_all[i * rows : (i + 1) * rows] = refs[0][...]
    x = x_all[...]
    gate = jnp.dot(x, gate_ref[...], preferred_element_type=jnp.float32)
    up = jnp.dot(x, up_ref[...], preferred_element_type=jnp.float32)
    hidden = activation(gate, up)
    out = jnp.dot(hidden, down_ref[...], preferred_element_type=jnp.float32).astype(jnp.bfloat16)
    row = 0
    for ref in out_refs:
        ref[...] = out[row : row + ref.shape[0]]
        row += ref.shape[0]


def side_kernel(mine_ref, met_ref, _, out_ref):
    rows = out_ref.shape[0]
    out_ref[...] = mine_ref[rows:].astype(jnp.float32) + met_ref[rows:].astype(jnp.float32)


def settle_kernel(mine_ref, met_ref, side_ref, out_ref):
    rows = out_ref.shape[0]
    total = mine_ref[:rows].astype(jnp.float32) + met_ref[:rows].astype(jnp.float32)
    out_ref[...] = total + side_ref[...].astype(jnp.float32)


def combine_kernel(settled_ref, side_ref, chosen_ref, weight_ref, out_hbm, out_ref, sems):
    chosen, weight = chosen_ref[...], weight_ref[...]
    steps = sems.shape[0]
    step = out_ref.shape[1] // steps
    copies = []
    for i in range(steps):
        part = slice(i * step, (i + 1) * step)
        total = settled_ref[:, part] + side_ref[:, part].astype(jnp.float32)
        out = lax.dot_general(
            chosen, total.astype(jnp.bfloat16), (((0,), (0,)), ((), ())),
            preferred_element_type=jnp.float32,
        )
        out_ref[:, part] = (weight * out).astype(jnp.bfloat16)
        copies.append(pltpu.make_async_copy(out_ref.at[:, part], out_hbm.at[:, part], sems.at[i]))
        copies[-1].start()
    for copy in copies:
        copy.wait()


def two_copies(
    tokens, expert_ids, replica, gate_weights, slot_table, gate_pieces, up_pieces, down_pieces
):
    devices = lax.axis_size("expert")
    count, width = tokens.shape
    rows = 2 * CAP
    hidden = gate_pieces.shape[2]
    bf16, f32 = jnp.bfloat16, jnp.float32
    in_hbm = pl.BlockSpec(memory_space=pltpu.HBM)
    in_vmem = pl.BlockSpec(memory_space=pltpu.VMEM)

    def partner(a):
        return lax.ppermute(a, "expert", [(i, i ^ 1) for i in range(devices)])

    def cross(a):
        return lax.ppermute(a, "expert", [(i, i ^ (4 if i % 2 else 2)) for i in range(devices)])

    def cross_back(a):
        return lax.ppermute(a, "expert", [(i, i ^ (2 if i % 2 else 4)) for i in range(devices)])

    def diagonal(a):
        return lax.ppermute(a, "expert", [(i, i ^ 6) for i in range(devices)])

    def add(a, b):
        return (a.astype(f32) + b.astype(f32)).astype(bf16)

    def cost(total):
        return pl.CostEstimate(
            flops=6 * total * width * hidden, bytes_accessed=6 * width * hidden, transcendentals=0
        )

    small = [expert_ids.T, replica.T, slot_table.T, gate_weights.T]
    own, chosen, weight = pl.pallas_call(
        pick_kernel,
        out_shape=[
            jax.ShapeDtypeStruct((rows, width), bf16),
            jax.ShapeDtypeStruct((rows, count), bf16),
            jax.ShapeDtypeStruct((count, 1), f32),
        ],
        in_specs=[in_hbm] * 5,
        scratch_shapes=[pltpu.VMEM(a.shape, a.dtype) for a in [tokens] + small]
        + [pltpu.SemaphoreType.DMA((5,))],
        compiler_params=within(56),
    )(tokens, *small)
    own_1 = partner(own)

    def load(done, *weights):
        return pl.pallas_call(
            load_kernel,
            out_shape=[jax.ShapeDtypeStruct(a.shape[1:], bf16) for a in weights],
            in_specs=[pl.BlockSpec(memory_space=pl.ANY)] + [in_hbm] * len(weights),
            out_specs=[in_vmem] * len(weights),
            scratch_shapes=[pltpu.SemaphoreType.DMA((len(weights), 8))],
            compiler_params=within(44),
            cost_estimate=cost(2 * rows),
        )(done, *[a[0] for a in weights])

    gate, up = load(own_1, gate_pieces, up_pieces)
    down = down_pieces[0]

    def after(done, *arrays):
        anywhere = pl.BlockSpec(memory_space=pl.ANY)
        return pl.pallas_call(
            hold_kernel,
            out_shape=[jax.ShapeDtypeStruct(a.shape, a.dtype) for a in arrays],
            in_specs=[anywhere] * (1 + len(arrays)),
            out_specs=[anywhere] * len(arrays),
            input_output_aliases={1 + i: i for i in range(len(arrays))},
            compiler_params=within(1),
        )(done, *arrays)

    def early(array, micros):
        anywhere = pl.BlockSpec(memory_space=pl.ANY)
        return pl.pallas_call(
            hold_kernel,
            out_shape=jax.ShapeDtypeStruct(array.shape, array.dtype),
            in_specs=[anywhere],
            out_specs=anywhere,
            input_output_aliases={0: 0},
            compiler_params=within(1),
            cost_estimate=pl.CostEstimate(
                flops=micros * 10**9, bytes_accessed=0, transcendentals=0
            ),
        )(array)

    def experts(outs, *arrays):
        blocks = len(arrays)
        return pl.pallas_call(
            functools.partial(expert_kernel, blocks),
            out_shape=[jax.ShapeDtypeStruct((rows * out, width), bf16) for out in outs],
            scratch_shapes=[pltpu.VMEM((rows * max(blocks, 5), width), bf16)],
            compiler_params=within(24),
            cost_estimate=cost(rows * blocks),
        )(*arrays, gate, up, down)

    near, = after(gate, cross(own))
    side_1, = after(gate, cross(own_1))
    far = cross_back(near)
    mine, near_other, other = experts((2, 1, 2), own, near, partner(near), own_1, side_1)
    near_met = partner(near_other)
    to_near = add(mine[rows:], near_met)
    side = early(partner(side_1), 10)
    far, = after(near_met, early(far, 10))
    last_mine, last_other = experts((2, 1), far, side, partner(far))
    to_far = add(last_mine[:rows], partner(last_other))
    other, = after(to_far, other)
    met = partner(other)
    passing = early(cross(to_far), 10)
    to_side = pl.pallas_call(
        side_kernel,
        out_shape=jax.ShapeDtypeStruct((rows, width), f32),
        in_specs=[in_vmem] * 2 + [pl.BlockSpec(memory_space=pl.ANY)],
        compiler_params=within(8),
        cost_estimate=cost(10 * rows),
    )(last_mine, met, to_far)
    got_side = cross_back((to_side + passing.astype(f32)).astype(bf16))
    got_near, = after(to_side, cross(to_near))
    settled = pl.pallas_call(
        settle_kernel,
        out_shape=jax.ShapeDtypeStruct((rows, width), f32),
        compiler_params=within(8),
    )(mine, met, got_near)
    return pl.pallas_call(
        combine_kernel,
        out_shape=jax.ShapeDtypeStruct((count, width), bf16),
        out_specs=pl.BlockSpec(memory_space=pl.ANY),
        scratch_shapes=[pltpu.VMEM((count, width), bf16), pltpu.SemaphoreType.DMA((4,))],
        compiler_params=within(24),
    )(settled, got_side, chosen, weight)


def solution(mesh):
    placed = (
        P(("groups", "expert"), None),
        P(("groups", "expert"), None),
        P(("groups", "expert"), None),
        P(("groups", "expert"), None),
        P("groups", None),
        P(("groups", "expert"), None, None),
        P(("groups", "expert"), None, None),
        P(("groups", "expert"), None, None),
    )
    return jax.shard_map(
        two_copies if mesh.shape["expert"] == 2 * PIECES else any_copies,
        mesh=mesh,
        in_specs=placed,
        out_specs=P(("groups", "expert"), None),
        check_vma=False,
    )
```
